32 devices in a mesh: grp: 4 (over y, core), loc: 8 (over z, x).
Axes of the slice: x: 2, y: 2, z: 4, core: 2. Of those that a mesh axis runs over, the one named last changes fastest.
Arguments:
- cavity_field: float32 [2, 256, 65536], P(None, ('grp', 'loc')), may hold values from -6 to 6
- direction: float32 [2, 2, 256, 65536], P(None, None, ('grp', 'loc')), may hold values from -6 to 6
- mode_degree: int32 [256], P(('grp', 'loc')), may hold values from 0 to 30
Outputs:
- preconditioned_product: float32 [2, 2, 256, 65536], P(None, None, ('grp', 'loc'))
The draws below stay inside these ranges and needn't reach their ends.
All inputs are finite; a program needn't handle non-finite values.
Results may differ from the reference program's by a relative error of at most 0.0043.
Values may be sent and summed in bfloat16 or wider, within the bound.
A program may use at most 256 MiB of HBM per device.

```python
import math
import jax
import jax.numpy as jnp
from jax import lax

MP = 16
MQ = 16
GSIDE = 64
DIRS = 2
M = 256
G = 4096
NT = 65536


def with_ends(values, stream_key, smallest, high):
    longest = values.shape.index(max(values.shape))
    spots = []
    for shift in (0, 1):
        where = [jax.random.randint(jax.random.fold_in(stream_key, axis), (), 0, length) for axis, length in enumerate(values.shape)]
        where[longest] = (where[longest] + shift) % values.shape[longest]
        spots.append(tuple(where))
    return values.at[spots[0]].set(smallest).at[spots[1]].set(high)


def level_of(rng, shape, cuts, smallest, high):
    def one(axis_at, shards_of):
        heights = jax.random.uniform(jax.random.fold_in(jax.random.fold_in(rng, 6), axis_at), (shards_of,), jnp.float32, smallest / len(cuts), high / len(cuts))
        return jnp.repeat(jnp.exp(heights), shape[axis_at] // shards_of).reshape((-1,) + (1,) * (len(shape) - axis_at - 1))

    factor_of = one(*cuts[0])
    for cut in cuts[1:]:
        factor_of = factor_of * one(*cut)
    return factor_of


def gaussian(key, shape, spread, limit, pieces=(), kind=jnp.bfloat16):
    gain = level_of(key, shape, pieces, -0.22, 0.18) if pieces else 1.0
    array = jax.random.normal(key, shape, jnp.float32) * spread * gain
    return jnp.minimum(jnp.maximum(array, -limit), limit).astype(kind)


def setup_inputs(seed: int = 0) -> dict:
    streams_of = jax.random.split(jax.random.key(seed), 4)
    cavity_field = gaussian(streams_of[0], (2, M, NT), 1.0, 6.0, ((1, 32),), jnp.float32)
    direction = gaussian(streams_of[1], (DIRS, 2, M, NT), 1.0, 6.0, ((2, 32),), jnp.float32)
    mode_degree = with_ends(jax.random.randint(streams_of[2], (M,), 0, MP + MQ - 1), jax.random.fold_in(streams_of[2], 1), 0, (MP + MQ - 1) - 1).astype(jnp.int32)
    return dict(cavity_field=cavity_field, direction=direction, mode_degree=mode_degree)


DETUNE = 4.0
BETA_STEP = 2.0
DISPERSION = 80.0
KERR_GAIN = 8.0

def hermite_grid():
    spacing = 16.0 / GSIDE
    position = (jnp.arange(GSIDE, dtype=jnp.float32) - (GSIDE - 1) / 2.0) * spacing
    ground = jnp.exp(-0.5 * position * position) * math.pi ** (-0.25)
    hermite = [ground, math.sqrt(2.0) * position * ground]
    for degree in range(1, max(MP, MQ) - 1):
        hermite.append(math.sqrt(2.0 / (degree + 1)) * position * hermite[degree] - math.sqrt(degree / (degree + 1.0)) * hermite[degree - 1])
    profiles = jnp.stack(hermite)
    outer = spacing * profiles[:MP][:, None, :, None] * profiles[:MQ][None, :, None, :]
    return jnp.transpose(outer.reshape(M, G)).astype(jnp.bfloat16)

def reference(cavity_field, direction, mode_degree):
    grid_b = lax.optimization_barrier(hermite_grid())
    grid_wide = grid_b.astype(jnp.float32)
    field_b = lax.optimization_barrier(cavity_field.astype(jnp.bfloat16)).astype(jnp.float32)
    dir_b = lax.optimization_barrier(direction.astype(jnp.bfloat16)).astype(jnp.float32)
    block_len = 2048 if NT % 2048 == 0 else NT

    def kerr_block(block_id):
        offset = (block_id * block_len).astype(jnp.int32)
        field_win = lax.dynamic_slice_in_dim(field_b, offset, block_len, 2)
        dir_win = lax.dynamic_slice_in_dim(dir_b, offset, block_len, 3)
        u_field = jnp.einsum('gm,cmt->cgt', grid_wide, field_win)
        w_field = jnp.einsum('gm,ecmt->ecgt', grid_wide, dir_win)
        u_real = u_field[0]
        u_imag = u_field[1]
        w_real = w_field[:, 0]
        w_imag = w_field[:, 1]
        cross = 2.0 * u_real * u_imag
        jac_real = (3.0 * u_real * u_real + u_imag * u_imag) * w_real + cross * w_imag
        jac_imag = cross * w_real + (u_real * u_real + 3.0 * u_imag * u_imag) * w_imag
        jacobian = lax.optimization_barrier(jnp.stack([jac_real, jac_imag], 1).astype(jnp.bfloat16))
        projected = jnp.einsum('gm,ecgt->ecmt', grid_wide, jacobian.astype(jnp.float32))
        kerr_b = jnp.stack([-KERR_GAIN * projected[:, 1], KERR_GAIN * projected[:, 0]], 1).astype(jnp.bfloat16)
        return lax.optimization_barrier(kerr_b).astype(jnp.float32)
    blocks = lax.map(kerr_block, jnp.arange(NT // block_len, dtype=jnp.int32))
    kerr_term = jnp.moveaxis(blocks, 0, 3).reshape(DIRS, 2, M, NT)
    frequency = jnp.arange(NT, dtype=jnp.int32)
    signed = jnp.where(frequency < NT // 2, frequency, frequency - NT).astype(jnp.float32)
    wavenumber = signed / (NT // 2)
    detuning = DETUNE - BETA_STEP * mode_degree.astype(jnp.float32)[:, None] + DISPERSION * (wavenumber * wavenumber)[None, :]
    linear = -1.0 - 1j * detuning
    precond = 2.0 + 1j * detuning
    spectrum_dir = jnp.fft.fft(direction[:, 0] + 1j * direction[:, 1], axis=-1)
    spectrum_kerr = jnp.fft.fft(kerr_term[:, 0] + 1j * kerr_term[:, 1], axis=-1)
    combined = (linear * spectrum_dir + spectrum_kerr) / precond
    result = jnp.fft.ifft(combined, axis=-1)
    return jnp.stack([jnp.real(result), jnp.imag(result)], 1).astype(jnp.float32)
```

```python
import functools
import math

import jax
import jax.numpy as jnp
import numpy as np
from jax import lax
from jax.experimental import pallas as pl
from jax.experimental.pallas import tpu as pltpu
from jax.sharding import PartitionSpec as P

MP = 16
MQ = 16
GSIDE = 64
NODES = 32
LEN = 256

DETUNE = 4.0
BETA_STEP = 2.0
DISPERSION = 80.0
KERR_GAIN = 8.0

CHUNKS = 2
AXES = ("grp", "loc")
MIB = 1 << 20


def node_table():
    spacing = 16.0 / GSIDE
    position = (np.arange(GSIDE) - (GSIDE - 1) / 2.0) * spacing
    root = spacing * np.exp(-position * position)
    basis = [root / np.linalg.norm(root)]
    diag, off = [], []
    for k in range(NODES):
        vec = position * basis[k]
        diag.append(vec @ basis[k])
        for _ in range(3):
            for prev in basis:
                vec = vec - (prev @ vec) * prev
        off.append(np.linalg.norm(vec))
        basis.append(vec / off[-1])
    jacobi = np.diag(diag) + np.diag(off[:-1], 1) + np.diag(off[:-1], -1)
    nodes, vectors = np.linalg.eigh(jacobi)
    weights = (root @ root) * vectors[0] ** 2
    nodes = 0.5 * (nodes - nodes[::-1])
    weights = 0.5 * (weights + weights[::-1])
    poly = [np.full(NODES, math.pi ** (-0.25)), math.sqrt(2.0) * nodes * math.pi ** (-0.25)]
    for degree in range(1, max(MP, MQ) - 1):
        poly.append(
            math.sqrt(2.0 / (degree + 1)) * nodes * poly[degree]
            - math.sqrt(degree / (degree + 1.0)) * poly[degree - 1]
        )
    side = np.stack(poly, 1) * (weights**0.25)[:, None]
    full = side[:, None, :MP, None] * side[None, :, None, :MQ]
    return full.reshape(NODES * NODES, MP * MQ)


def prep_kernel(chunks, dests, field_ref, dir_ref, *out_refs):
    span = field_ref.shape[2] // dests
    part = span // chunks
    for d in range(dests):
        for j in range(chunks):
            where = pl.ds(d * span + j * part, part)
            for c in range(2):
                out_refs[j][d, c] = field_ref[c, :, where].astype(jnp.bfloat16)
                for e in range(dir_ref.shape[0]):
                    out_refs[j][d, 2 + 2 * e + c] = dir_ref[e, c, :, where].astype(jnp.bfloat16)


def prep(cavity_field, direction, devices, chunks):
    dirs, _, modes, time_all = direction.shape
    sets = 2 * (dirs + 1)
    span = time_all // devices
    dests = 4
    part = span // chunks
    return pl.pallas_call(
        functools.partial(prep_kernel, chunks, dests),
        grid=(devices // dests,),
        in_specs=[
            pl.BlockSpec((2, modes, dests * span), lambda i: (0, 0, i)),
            pl.BlockSpec((dirs, 2, modes, dests * span), lambda i: (0, 0, 0, i)),
        ],
        out_specs=[pl.BlockSpec((dests, sets, modes, part), lambda i: (i, 0, 0, 0))] * chunks,
        out_shape=[jax.ShapeDtypeStruct((devices, sets, modes, part), jnp.bfloat16)] * chunks,
        compiler_params=pltpu.CompilerParams(vmem_limit_bytes=40 * MIB),
        name="prep",
    )(cavity_field, direction)


def halves(values):
    high = values.astype(jnp.bfloat16)
    return high, (values - high.astype(jnp.float32)).astype(jnp.bfloat16)


def dot16(left, right):
    return jnp.dot(left, right, preferred_element_type=jnp.float32)


def kerr_kernel(table_ref, back_ref, x_ref, out_ref):
    groups, sets, rows, cols = x_ref.shape
    modes = groups * rows
    points = table_ref.shape[1]
    step = 256
    planes = [
        x_ref[:, s].astype(jnp.float32).reshape(modes, cols).astype(jnp.bfloat16)
        for s in range(sets)
    ]
    dirs = sets // 2 - 1
    totals = [jnp.zeros((modes, cols), jnp.float32) for _ in range(2 * dirs)]
    for g in range(0, points, step):
        at = slice(g, g + step)
        vals = [dot16(table_ref[0, at, :], p) + dot16(table_ref[1, at, :], p) for p in planes]
        u_real, u_imag = vals[0], vals[1]
        real_sq = u_real * u_real
        imag_sq = u_imag * u_imag
        lead = 3.0 * real_sq + imag_sq
        tail = real_sq + 3.0 * imag_sq
        cross = 2.0 * u_real * u_imag
        back_high, back_low = back_ref[0, :, at], back_ref[1, :, at]
        for e in range(dirs):
            w_real, w_imag = vals[2 + 2 * e], vals[3 + 2 * e]
            jac = (lead * w_real + cross * w_imag, cross * w_real + tail * w_imag)
            for c in range(2):
                high, low = halves(jac[c])
                totals[2 * e + c] += (
                    dot16(back_high, high) + dot16(back_low, high) + dot16(back_high, low)
                )
    for e in range(dirs):
        out_ref[:, 2 * e, 0] = (
            (-KERR_GAIN * totals[2 * e + 1]).reshape(groups, rows, cols).astype(jnp.bfloat16)
        )
        out_ref[:, 2 * e + 1, 0] = (
            (KERR_GAIN * totals[2 * e]).reshape(groups, rows, cols).astype(jnp.bfloat16)
        )


def kerr(table, back, x):
    groups, sets, rows, cols = x.shape
    _, points, modes = table.shape
    blocks = cols // LEN
    outs = sets - 2
    return pl.pallas_call(
        kerr_kernel,
        grid=(blocks,),
        in_specs=[
            pl.BlockSpec((2, points, modes), lambda i: (0, 0, 0)),
            pl.BlockSpec((2, modes, points), lambda i: (0, 0, 0)),
            pl.BlockSpec((groups, sets, rows, LEN), lambda i: (0, 0, 0, i)),
        ],
        out_specs=pl.BlockSpec((groups, outs, 1, rows, LEN), lambda i: (0, 0, i, 0, 0)),
        out_shape=jax.ShapeDtypeStruct((groups, outs, blocks, rows, LEN), jnp.bfloat16),
        compiler_params=pltpu.CompilerParams(vmem_limit_bytes=40 * MIB),
        cost_estimate=pl.CostEstimate(
            flops=2 * (2 * sets + 3 * outs) * points * modes * cols,
            bytes_accessed=2 * (sets + outs) * modes * cols,
            transcendentals=0,
        ),
        name="kerr",
    )(table, back, x)


def split_table(values):
    high = np.asarray(values, jnp.bfloat16)
    low = np.asarray(values - high.astype(np.float64), jnp.bfloat16)
    return jnp.asarray(np.stack([high, low]))


def dot_left(table_ref, values):
    high, low = halves(values)
    return dot16(table_ref[0], high) + dot16(table_ref[1], high) + dot16(table_ref[0], low)


def dot_right(values, table_ref):
    high, low = halves(values)
    return dot16(high, table_ref[0]) + dot16(high, table_ref[1]) + dot16(low, table_ref[0])


def filter_kernel(chunks, degree_ref, left_ref, right_ref, left_inv_ref, right_inv_ref, twc_ref, tws_ref, disp_ref,
                  dir_ref, *rest):
    kerr_refs = rest[:chunks]
    out_ref, wide, rows = rest[chunks:]
    modes = dir_ref.shape[2]
    sources, _, blocks = kerr_refs[0].shape[:3]
    mode = pl.program_id(1)

    @pl.when(mode == 0)
    def _():
        def gather(src, carry):
            for j in range(chunks):
                for c in range(2):
                    for b in range(blocks):
                        at = (src * chunks + j) * blocks + b
                        lanes = pl.ds(pl.multiple_of(at * LEN, LEN), LEN)
                        wide[c, at] = dir_ref[0, c, :, lanes] + kerr_refs[j][src, c, b].astype(jnp.float32)
            return carry

        lax.fori_loop(0, sources, gather, 0)
        for m in range(modes):
            for c in range(2):
                rows[c, m] = wide[c, :, m, :]

    tw_cos = twc_ref[...]
    tw_sin = tws_ref[...]
    pair = jnp.concatenate([rows[0, mode], rows[1, mode]], 0)
    step = dot_left(left_ref, pair)
    step_real, step_imag = step[:LEN], step[LEN:]
    turned = jnp.concatenate(
        [
            step_real * tw_cos + step_imag * tw_sin,
            step_imag * tw_cos - step_real * tw_sin,
        ],
        1,
    )
    spec = dot_right(turned, right_ref)
    spec_real, spec_imag = spec[:, :LEN], spec[:, LEN:]
    phase = disp_ref[...] - BETA_STEP * degree_ref[mode].astype(jnp.float32)
    scale = (1.0 / (LEN * LEN)) / (4.0 + phase * phase)
    inv_real = 2.0 * scale
    inv_imag = -phase * scale
    mixed = jnp.concatenate(
        [
            inv_real * spec_real - inv_imag * spec_imag,
            inv_real * spec_imag + inv_imag * spec_real,
        ],
        1,
    )
    back = dot_right(mixed, right_inv_ref)
    back_real, back_imag = back[:, :LEN], back[:, LEN:]
    unturned = jnp.concatenate(
        [
            back_real * tw_cos - back_imag * tw_sin,
            back_imag * tw_cos + back_real * tw_sin,
        ],
        0,
    )
    done = dot_left(left_inv_ref, unturned)
    rows[0, mode] = done[:LEN]
    rows[1, mode] = done[LEN:]

    @pl.when(mode == modes - 1)
    def _():
        for m in range(modes):
            for c in range(2):
                wide[c, :, m, :] = rows[c, m]

        def scatter(i, carry):
            for b in range(8):
                at = i * 8 + b
                lanes = pl.ds(pl.multiple_of(at * LEN, LEN), LEN)
                for c in range(2):
                    out_ref[0, c, :, lanes] = wide[c, at] - dir_ref[0, c, :, lanes]
            return carry

        lax.fori_loop(0, LEN // 8, scatter, 0)


def filter_tables():
    idx = np.arange(LEN)
    angles = 2.0 * np.pi / LEN * (idx[:, None] * idx[None, :] % LEN)
    cos, sin = np.cos(angles), np.sin(angles)
    left = np.block([[cos, sin], [-sin, cos]])
    right = np.block([[cos, -sin], [sin, cos]])
    turn = 2.0 * np.pi / (LEN * LEN) * (idx[:, None] * idx[None, :])
    frequency = idx[:, None] + LEN * idx[None, :]
    half = LEN * LEN // 2
    kappa = np.where(frequency < half, frequency, frequency - 2 * half) / half
    mats = [split_table(t) for t in (left, right, right, left)]
    rest = [np.cos(turn), np.sin(turn), DETUNE + DISPERSION * kappa * kappa]
    return mats + [jnp.asarray(t, jnp.float32) for t in rest]


def precondition(mode_degree, direction, kerr_parts):
    dirs, _, modes, time_all = direction.shape
    chunks = len(kerr_parts)
    sources, _, blocks = kerr_parts[0].shape[:3]
    big = pl.BlockSpec((2, 2 * LEN, 2 * LEN), lambda e, m: (0, 0, 0))
    small = pl.BlockSpec((LEN, LEN), lambda e, m: (0, 0))
    wave = pl.BlockSpec((1, 2, modes, time_all), lambda e, m: (e, 0, 0, 0))
    part = pl.BlockSpec((sources, 2, blocks, modes, LEN), lambda e, m: (0, e, 0, 0, 0))
    return pl.pallas_call(
        functools.partial(filter_kernel, chunks),
        grid=(dirs, modes),
        in_specs=[pl.BlockSpec(memory_space=pltpu.SMEM)]
        + [big] * 4
        + [small] * 3
        + [wave]
        + [part] * chunks,
        out_specs=wave,
        out_shape=jax.ShapeDtypeStruct(direction.shape, jnp.float32),
        scratch_shapes=[
            pltpu.VMEM((2, LEN, modes, LEN), jnp.float32),
            pltpu.VMEM((2, modes, LEN, LEN), jnp.float32),
        ],
        compiler_params=pltpu.CompilerParams(vmem_limit_bytes=56 * MIB),
        name="precondition",
    )(mode_degree, *filter_tables(), direction, *kerr_parts)


def local(devices, cavity_field, direction, mode_degree):
    modes = direction.shape[2]
    table = node_table()
    forward = split_table(table)
    back = split_table(table.T)
    fold = max(1, 8 // modes)
    kerr_parts = []
    for x in prep(cavity_field, direction, devices, CHUNKS):
        x = lax.all_to_all(x, AXES, split_axis=0, concat_axis=0, tiled=True)
        if fold > 1:
            n, sets, r, cols = x.shape
            x = x.reshape(n // fold, fold, sets, r, cols).transpose(0, 2, 1, 3, 4)
            x = x.reshape(n // fold, sets, fold * r, cols)
        y = kerr(forward, back, x)
        if fold > 1:
            n, outs, blocks, r, cols = y.shape
            y = y.reshape(n, outs, blocks, fold, r // fold, cols).transpose(0, 3, 1, 2, 4, 5)
            y = y.reshape(n * fold, outs, blocks, r // fold, cols)
        kerr_parts.append(lax.all_to_all(y, AXES, split_axis=0, concat_axis=0, tiled=True))
    return precondition(mode_degree, direction, kerr_parts)


def solution(mesh):
    placed = (P(None, AXES, None), P(None, None, AXES, None), P(AXES))
    return jax.shard_map(
        functools.partial(local, mesh.size),
        mesh=mesh,
        in_specs=placed,
        out_specs=P(None, None, AXES, None),
        check_vma=False,
    )
```

```python
import functools
import math

import jax
import jax.numpy as jnp
import numpy as np
from jax import lax
from jax.experimental import pallas as pl
from jax.experimental.pallas import tpu as pltpu
from jax.sharding import PartitionSpec as P

MP = 16
MQ = 16
GSIDE = 64
NODES = 32
LEN = 256

DETUNE = 4.0
BETA_STEP = 2.0
DISPERSION = 80.0
KERR_GAIN = 8.0

CHUNKS = 2
AXES = ("grp", "loc")
MIB = 1 << 20


def node_table():
    spacing = 16.0 / GSIDE
    position = (np.arange(GSIDE) - (GSIDE - 1) / 2.0) * spacing
    root = spacing * np.exp(-position * position)
    basis = [root / np.linalg.norm(root)]
    diag, off = [], []
    for k in range(NODES):
        vec = position * basis[k]
        diag.append(vec @ basis[k])
        for _ in range(3):
            for prev in basis:
                vec = vec - (prev @ vec) * prev
        off.append(np.linalg.norm(vec))
        basis.append(vec / off[-1])
    jacobi = np.diag(diag) + np.diag(off[:-1], 1) + np.diag(off[:-1], -1)
    nodes, vectors = np.linalg.eigh(jacobi)
    weights = (root @ root) * vectors[0] ** 2
    nodes = 0.5 * (nodes - nodes[::-1])
    weights = 0.5 * (weights + weights[::-1])
    poly = [np.full(NODES, math.pi ** (-0.25)), math.sqrt(2.0) * nodes * math.pi ** (-0.25)]
    for degree in range(1, max(MP, MQ) - 1):
        poly.append(
            math.sqrt(2.0 / (degree + 1)) * nodes * poly[degree]
            - math.sqrt(degree / (degree + 1.0)) * poly[degree - 1]
        )
    side = np.stack(poly, 1) * (weights**0.25)[:, None]
    full = side[:, None, :MP, None] * side[None, :, None, :MQ]
    return full.reshape(NODES * NODES, MP * MQ)


def prep_kernel(chunks, dests, field_ref, dir_ref, *out_refs):
    span = field_ref.shape[2] // dests
    part = span // chunks
    for d in range(dests):
        for j in range(chunks):
            where = pl.ds(d * span + j * part, part)
            for c in range(2):
                out_refs[j][d, c] = field_ref[c, :, where].astype(jnp.bfloat16)
                for e in range(dir_ref.shape[0]):
                    out_refs[j][d, 2 + 2 * e + c] = dir_ref[e, c, :, where].astype(jnp.bfloat16)


def prep(cavity_field, direction, devices, chunks):
    dirs, _, modes, time_all = direction.shape
    sets = 2 * (dirs + 1)
    span = time_all // devices
    dests = 4
    part = span // chunks
    return pl.pallas_call(
        functools.partial(prep_kernel, chunks, dests),
        grid=(devices // dests,),
        in_specs=[
            pl.BlockSpec((2, modes, dests * span), lambda i: (0, 0, i)),
            pl.BlockSpec((dirs, 2, modes, dests * span), lambda i: (0, 0, 0, i)),
        ],
        out_specs=[pl.BlockSpec((dests, sets, modes, part), lambda i: (i, 0, 0, 0))] * chunks,
        out_shape=[jax.ShapeDtypeStruct((devices, sets, modes, part), jnp.bfloat16)] * chunks,
        compiler_params=pltpu.CompilerParams(vmem_limit_bytes=40 * MIB),
        name="prep",
    )(cavity_field, direction)


def halves(values):
    high = values.astype(jnp.bfloat16)
    return high, (values - high.astype(jnp.float32)).astype(jnp.bfloat16)


def dot16(left, right):
    return jnp.dot(left, right, preferred_element_type=jnp.float32)


def kerr_kernel(table_ref, back_ref, x_ref, *out_refs):
    groups, sets, rows, cols = x_ref.shape
    modes = groups * rows
    points = table_ref.shape[1]
    step = 256
    planes = [
        x_ref[:, s].astype(jnp.float32).reshape(modes, cols).astype(jnp.bfloat16)
        for s in range(sets)
    ]
    dirs = sets // 2 - 1
    totals = [jnp.zeros((modes, cols), jnp.float32) for _ in range(2 * dirs)]
    for g in range(0, points, step):
        at = slice(g, g + step)
        vals = [dot16(table_ref[0, at, :], p) + dot16(table_ref[1, at, :], p) for p in planes]
        u_real, u_imag = vals[0], vals[1]
        real_sq = u_real * u_real
        imag_sq = u_imag * u_imag
        lead = 3.0 * real_sq + imag_sq
        tail = real_sq + 3.0 * imag_sq
        cross = 2.0 * u_real * u_imag
        back_high, back_low = back_ref[0, :, at], back_ref[1, :, at]
        for e in range(dirs):
            w_real, w_imag = vals[2 + 2 * e], vals[3 + 2 * e]
            jac = (lead * w_real + cross * w_imag, cross * w_real + tail * w_imag)
            for c in range(2):
                high, low = halves(jac[c])
                totals[2 * e + c] += (
                    dot16(back_high, high) + dot16(back_low, high) + dot16(back_high, low)
                )
    for e in range(dirs):
        at = 2 * (e % (dirs // len(out_refs)))
        out_ref = out_refs[e * len(out_refs) // dirs]
        out_ref[:, at, 0] = (
            (-KERR_GAIN * totals[2 * e + 1]).reshape(groups, rows, cols).astype(jnp.bfloat16)
        )
        out_ref[:, at + 1, 0] = (
            (KERR_GAIN * totals[2 * e]).reshape(groups, rows, cols).astype(jnp.bfloat16)
        )


def kerr(table, back, x, pieces):
    groups, sets, rows, cols = x.shape
    _, points, modes = table.shape
    blocks = cols // LEN
    outs = sets - 2
    return pl.pallas_call(
        kerr_kernel,
        grid=(blocks,),
        in_specs=[
            pl.BlockSpec((2, points, modes), lambda i: (0, 0, 0)),
            pl.BlockSpec((2, modes, points), lambda i: (0, 0, 0)),
            pl.BlockSpec((groups, sets, rows, LEN), lambda i: (0, 0, 0, i)),
        ],
        out_specs=[pl.BlockSpec((groups, outs // pieces, 1, rows, LEN), lambda i: (0, 0, i, 0, 0))]
        * pieces,
        out_shape=[jax.ShapeDtypeStruct((groups, outs // pieces, blocks, rows, LEN), jnp.bfloat16)]
        * pieces,
        compiler_params=pltpu.CompilerParams(vmem_limit_bytes=40 * MIB),
        cost_estimate=pl.CostEstimate(
            flops=2 * (2 * sets + 3 * outs) * points * modes * cols,
            bytes_accessed=2 * (sets + outs) * modes * cols,
            transcendentals=0,
        ),
        name="kerr",
    )(table, back, x)


def split_table(values):
    high = np.asarray(values, jnp.bfloat16)
    low = np.asarray(values - high.astype(np.float64), jnp.bfloat16)
    return jnp.asarray(np.stack([high, low]))


def dot_left(table_ref, values):
    high, low = halves(values)
    return dot16(table_ref[0], high) + dot16(table_ref[1], high) + dot16(table_ref[0], low)


def dot_right(values, table_ref):
    high, low = halves(values)
    return dot16(high, table_ref[0]) + dot16(high, table_ref[1]) + dot16(low, table_ref[0])


def filter_kernel(chunks, degree_ref, left_ref, right_ref, left_inv_ref, right_inv_ref, twc_ref, tws_ref, disp_ref,
                  dir_ref, *rest):
    kerr_refs = rest[:chunks]
    out_ref, wide, rows = rest[-3:]
    modes = dir_ref.shape[2]
    sources, _, blocks = kerr_refs[0].shape[:3]
    mode = pl.program_id(0)

    @pl.when(mode == 0)
    def _():
        def gather(src, carry):
            for j in range(chunks):
                for c in range(2):
                    for b in range(blocks):
                        at = (src * chunks + j) * blocks + b
                        lanes = pl.ds(pl.multiple_of(at * LEN, LEN), LEN)
                        wide[c, at] = dir_ref[0, c, :, lanes] + kerr_refs[j][src, c, b].astype(jnp.float32)
            return carry

        lax.fori_loop(0, sources, gather, 0)
        for m in range(modes):
            for c in range(2):
                rows[c, m] = wide[c, :, m, :]

    tw_cos = twc_ref[...]
    tw_sin = tws_ref[...]
    pair = jnp.concatenate([rows[0, mode], rows[1, mode]], 0)
    step = dot_left(left_ref, pair)
    step_real, step_imag = step[:LEN], step[LEN:]
    turned = jnp.concatenate(
        [
            step_real * tw_cos + step_imag * tw_sin,
            step_imag * tw_cos - step_real * tw_sin,
        ],
        1,
    )
    spec = dot_right(turned, right_ref)
    spec_real, spec_imag = spec[:, :LEN], spec[:, LEN:]
    phase = disp_ref[...] - BETA_STEP * degree_ref[mode].astype(jnp.float32)
    scale = (1.0 / (LEN * LEN)) / (4.0 + phase * phase)
    inv_real = 2.0 * scale
    inv_imag = -phase * scale
    mixed = jnp.concatenate(
        [
            inv_real * spec_real - inv_imag * spec_imag,
            inv_real * spec_imag + inv_imag * spec_real,
        ],
        1,
    )
    back = dot_right(mixed, right_inv_ref)
    back_real, back_imag = back[:, :LEN], back[:, LEN:]
    unturned = jnp.concatenate(
        [
            back_real * tw_cos - back_imag * tw_sin,
            back_imag * tw_cos + back_real * tw_sin,
        ],
        0,
    )
    done = dot_left(left_inv_ref, unturned)
    rows[0, mode] = done[:LEN]
    rows[1, mode] = done[LEN:]

    @pl.when(mode == modes - 1)
    def _():
        for m in range(modes):
            for c in range(2):
                wide[c, :, m, :] = rows[c, m]

        def scatter(i, carry):
            for b in range(8):
                at = i * 8 + b
                lanes = pl.ds(pl.multiple_of(at * LEN, LEN), LEN)
                for c in range(2):
                    out_ref[0, c, :, lanes] = wide[c, at] - dir_ref[0, c, :, lanes]
            return carry

        lax.fori_loop(0, LEN // 8, scatter, 0)


def filter_tables():
    idx = np.arange(LEN)
    angles = 2.0 * np.pi / LEN * (idx[:, None] * idx[None, :] % LEN)
    cos, sin = np.cos(angles), np.sin(angles)
    left = np.block([[cos, sin], [-sin, cos]])
    right = np.block([[cos, -sin], [sin, cos]])
    turn = 2.0 * np.pi / (LEN * LEN) * (idx[:, None] * idx[None, :])
    frequency = idx[:, None] + LEN * idx[None, :]
    half = LEN * LEN // 2
    kappa = np.where(frequency < half, frequency, frequency - 2 * half) / half
    mats = [split_table(t) for t in (left, right, right, left)]
    rest = [np.cos(turn), np.sin(turn), DETUNE + DISPERSION * kappa * kappa]
    return mats + [jnp.asarray(t, jnp.float32) for t in rest]


def precondition(mode_degree, direction, which, kerr_parts, result):
    dirs, _, modes, time_all = direction.shape
    chunks = len(kerr_parts)
    sources, _, blocks = kerr_parts[0].shape[:3]
    big = pl.BlockSpec((2, 2 * LEN, 2 * LEN), lambda m: (0, 0, 0))
    small = pl.BlockSpec((LEN, LEN), lambda m: (0, 0))
    wave = pl.BlockSpec((1, 2, modes, time_all), lambda m: (which, 0, 0, 0))
    parts = [
        pl.BlockSpec(
            (sources, 2, blocks, modes, LEN),
            lambda m, at=which if p.shape[1] == 2 * dirs else 0: (0, at, 0, 0, 0),
        )
        for p in kerr_parts
    ]
    extra = [] if result is None else [result]
    operands = [mode_degree, *filter_tables(), direction, *kerr_parts, *extra]
    return pl.pallas_call(
        functools.partial(filter_kernel, chunks),
        grid=(modes,),
        in_specs=[pl.BlockSpec(memory_space=pltpu.SMEM)]
        + [big] * 4
        + [small] * 3
        + [wave]
        + parts
        + [pl.BlockSpec(memory_space=pl.ANY)] * len(extra),
        out_specs=wave,
        out_shape=jax.ShapeDtypeStruct(direction.shape, jnp.float32),
        scratch_shapes=[
            pltpu.VMEM((2, LEN, modes, LEN), jnp.float32),
            pltpu.VMEM((2, modes, LEN, LEN), jnp.float32),
        ],
        compiler_params=pltpu.CompilerParams(vmem_limit_bytes=56 * MIB),
        input_output_aliases={len(operands) - 1: 0} if extra else {},
        cost_estimate=pl.CostEstimate(
            flops=24 * modes * (2 * LEN) ** 2 * LEN,
            bytes_accessed=20 * modes * time_all,
            transcendentals=0,
        ),
        name="precondition",
    )(*operands)


def local(devices, cavity_field, direction, mode_degree):
    modes = direction.shape[2]
    table = node_table()
    forward = split_table(table)
    back = split_table(table.T)
    fold = max(1, 8 // modes)
    dirs = direction.shape[0]
    parts = prep(cavity_field, direction, devices, CHUNKS)
    kerr_parts = []
    for j, x in enumerate(parts):
        x = lax.all_to_all(x, AXES, split_axis=0, concat_axis=0, tiled=True)
        if fold > 1:
            n, sets, r, cols = x.shape
            x = x.reshape(n // fold, fold, sets, r, cols).transpose(0, 2, 1, 3, 4)
            x = x.reshape(n // fold, sets, fold * r, cols)
        sent = []
        for y in kerr(forward, back, x, dirs if j == len(parts) - 1 else 1):
            if fold > 1:
                n, outs, blocks, r, cols = y.shape
                y = y.reshape(n, outs, blocks, fold, r // fold, cols).transpose(0, 3, 1, 2, 4, 5)
                y = y.reshape(n * fold, outs, blocks, r // fold, cols)
            sent.append(lax.all_to_all(y, AXES, split_axis=0, concat_axis=0, tiled=True))
        kerr_parts.append(sent)
    result = None
    for e in range(dirs):
        arrived = [sent[e % len(sent)] for sent in kerr_parts]
        result = precondition(mode_degree, direction, e, arrived, result)
    return result


def solution(mesh):
    placed = (P(None, AXES, None), P(None, None, AXES, None), P(AXES))
    return jax.shard_map(
        functools.partial(local, mesh.size),
        mesh=mesh,
        in_specs=placed,
        out_specs=P(None, None, AXES, None),
        check_vma=False,
    )
```
